128 devices in a mesh: dp: 8 (over z, y_hi), mp: 16 (over y_lo, x, core).
Axes of the slice: x: 4, y: 4 (y_hi: 2, y_lo: 2; y = y_hi * 2 + y_lo), z: 4, core: 2. Of those that a mesh axis runs over, the one named last changes fastest.
Arguments:
- grads: bfloat16 [8, 128, 8192, 128], P('dp', None, 'mp')
- momentum: bfloat16 [8, 16, 2, 8192, 128], P('dp', 'mp'), may hold values from -6 to 6
- owner_table: int32 [8, 16, 2], P('dp'), may hold values from 0 to 16, as said below
Outputs:
- update: bfloat16 [128, 8192, 128], P('dp', 'mp')
- new_momentum: bfloat16 [8, 16, 2, 8192, 128], P('dp', 'mp')
The draws below stay inside these ranges and needn't reach their ends.
Inputs may be any that keep to these rules, and one draw needn't show every extreme that they name: For each index d of dp, the 16 x 2 entries owner_table[d] name each matrix 0 to 15 of the group exactly once, and every other slot holds 16, meaning empty. In every group some owner has all 2 slots filled.
All inputs are finite; a program needn't handle non-finite values.
Results may differ from the reference program's by a relative error of at most 0.025.
Values may be sent and summed in bfloat16 or wider, within the bound.
No kernel may reach another device: no remote copies, remote signals or barrier semaphores. Data moves between devices by JAX's collectives and lax.ppermute only.
A program may use at most 128 MiB of HBM per device.

```python
import math
import jax
import jax.numpy as jnp
from jax import lax

ROWS = 8192
HEAD = 128
ITERS = 2
MATRICES = 128
GROUP_MATS = 16
SLOTS = 2
N_DP = 8
N_MP = 16


def draw_grads(key, part):
    key = jax.random.fold_in(key, 5)
    key_rows, key_cols, key_noise = jax.random.split(key, 3)
    row_scale = jnp.exp(jax.random.uniform(key_rows, (1, MATRICES, ROWS, 1), jnp.float32) * math.log(10.0))
    col_scale = jnp.exp(jax.random.uniform(key_cols, (1, MATRICES, 1, HEAD), jnp.float32) * math.log(10.0))
    noise = jax.random.normal(key_noise, (N_DP, MATRICES, ROWS, HEAD), jnp.float32)
    values = noise * row_scale * col_scale * 0.1
    return values.astype(jnp.bfloat16)


def owner_group(key):
    key_order, key_full, key_ids = jax.random.split(key, 3)
    slot_total = N_MP * SLOTS
    scores = jax.random.permutation(key_order, slot_total).astype(jnp.int32)
    full_owner = jax.random.randint(key_full, (), 0, N_MP, dtype=jnp.int32)
    owner_of = (jnp.arange(slot_total, dtype=jnp.int32) // SLOTS).astype(jnp.int32)
    scores = scores + slot_total * (owner_of == full_owner).astype(jnp.int32)
    order = jnp.argsort(-scores, stable=True)
    matrix_ids = jax.random.permutation(key_ids, GROUP_MATS).astype(jnp.int32)
    filled = jnp.full((slot_total,), GROUP_MATS, jnp.int32).at[order[:GROUP_MATS]].set(matrix_ids)
    return filled.reshape(N_MP, SLOTS)


def draw_owner_table(key, part):
    key = jax.random.fold_in(key, 11)
    return jax.vmap(owner_group)(jax.random.split(key, N_DP))


def block_scale(key, shape, cuts, least, high):
    factor_of = 1.0
    for dim, blocks in cuts:
        draws = jax.random.uniform(jax.random.fold_in(jax.random.fold_in(key, 6), dim), (blocks,), jnp.float32, least / len(cuts), high / len(cuts))
        factor_of = factor_of * jnp.repeat(jnp.exp(draws), shape[dim] // blocks).reshape((-1,) + (1,) * (len(shape) - 1 - dim))
    return factor_of


def gaussian(own_key, shape, deviation, most, cuts=(), held_as=jnp.bfloat16):
    drawn = deviation * jax.random.normal(own_key, shape, jnp.float32)
    if cuts:
        drawn = drawn * block_scale(own_key, shape, cuts, -0.22, 0.18)
    return jnp.clip(drawn, -most, most).astype(held_as)


def setup_inputs(seed: int = 0) -> dict:
    key_list = jax.random.split(jax.random.key(seed), 4)
    grads = draw_grads(jax.random.fold_in(key_list[3], 71), 0)
    momentum = gaussian(key_list[1], (N_DP, N_MP, SLOTS, ROWS, HEAD), 1.0, 6.0, ((0, 8), (1, 16)))
    owner_table = draw_owner_table(jax.random.fold_in(key_list[3], 71), 0)
    return {"grads": grads, "momentum": momentum, "owner_table": owner_table}


momentum_rate = 0.95
coef_first = 3.4445
coef_second = -4.775
coef_third = 2.0315
norm_eps = 1e-07

def locate(owners, group_count):
    flat_owners = owners.reshape(-1)
    index = jnp.arange(flat_owners.shape[0], dtype=jnp.int32)
    wanted = jnp.arange(group_count, dtype=jnp.int32)
    hits = flat_owners[None, :] == wanted[:, None]
    return lax.optimization_barrier(jnp.sum(jnp.where(hits, index[None, :], 0), axis=1)).astype(jnp.int32)

def polish(mixed):
    length = jnp.sqrt(jnp.sum(mixed * mixed))
    iterate = (mixed / (length + norm_eps)).astype(jnp.bfloat16)
    high = lax.Precision.HIGHEST
    for iteration in range(ITERS):
        wide = iterate.astype(jnp.float32)
        gram = jnp.dot(wide.T, wide, precision=high).astype(jnp.bfloat16)
        gram_wide = gram.astype(jnp.float32)
        square = jnp.dot(gram_wide, gram_wide, precision=high)
        poly = (coef_second * gram_wide + coef_third * square).astype(jnp.bfloat16)
        iterate = (coef_first * wide + jnp.dot(wide, poly.astype(jnp.float32), precision=high)).astype(jnp.bfloat16)
    return (math.sqrt(ROWS) * iterate.astype(jnp.float32)).astype(jnp.bfloat16)

def reference(grads, momentum, owner_table):
    summed = grads[0].astype(jnp.float32)
    for replica in range(1, N_DP):
        summed = summed + grads[replica].astype(jnp.float32)
    updates = []
    buffers = []
    for group in range(N_DP):
        block = summed[group * GROUP_MATS:(group + 1) * GROUP_MATS]
        owners = owner_table[group]
        slot_grad = jnp.take(block, owners.reshape(-1), axis=0, mode='fill', fill_value=0.0)
        stored = momentum[group].reshape(N_MP * SLOTS, ROWS, HEAD).astype(jnp.float32)
        renewed = (momentum_rate * stored + slot_grad).astype(jnp.bfloat16)
        mixed = slot_grad + momentum_rate * renewed.astype(jnp.float32)
        placed = locate(owners, GROUP_MATS)
        chosen = jnp.take(mixed, placed, axis=0)
        updates.append(lax.map(polish, chosen))
        buffers.append(renewed.reshape(N_MP, SLOTS, ROWS, HEAD))
    return (jnp.concatenate(updates, axis=0), jnp.stack(buffers, axis=0))
```

```python
import math

import jax
import jax.numpy as jnp
from jax import lax
from jax.experimental import pallas as pl
from jax.experimental.pallas import tpu as pltpu
from jax.sharding import PartitionSpec as P

ROWS = 8192
HEAD = 128
ITERS = 2

momentum_rate = 0.95
coef_first = 3.4445
coef_second = -4.775
coef_third = 2.0315
norm_eps = 1e-07

Z_SIZE = 4
Y_SIZE = 2
CHUNKS = ((0, 256, False), (256, 128, False), (384, 128, True))
VMEM = 48 * 1024 * 1024


def params():
    return pltpu.CompilerParams(vmem_limit_bytes=VMEM)


def z_groups():
    return [[z * Y_SIZE + y for z in range(Z_SIZE)] for y in range(Y_SIZE)]


def swap_y(x):
    return lax.ppermute(x, "dp", [(i, i ^ 1) for i in range(Z_SIZE * Y_SIZE)])


def scatter_z(x):
    return lax.psum_scatter(
        x, "dp", scatter_dimension=0, tiled=True, axis_index_groups=z_groups()
    )


def exchange(x):
    return lax.all_to_all(x, "mp", split_axis=0, concat_axis=0, tiled=True)


def add_pair(half, whole, received, first_row, rows):
    def body(half_ref, whole_ref, received_ref, out_ref):
        out_ref[0] = (
            whole_ref[0, 0].astype(jnp.float32) + received_ref[0].astype(jnp.float32)
        ).astype(jnp.bfloat16)

    mats = whole.shape[2]
    per = 8
    return pl.pallas_call(
        body,
        grid_spec=pltpu.PrefetchScalarGridSpec(
            num_scalar_prefetch=1,
            grid=(Z_SIZE, mats // per),
            in_specs=[
                pl.BlockSpec((1, 1, per, rows, HEAD), lambda z, k, h: (z, h[0], k, first_row // rows, 0)),
                pl.BlockSpec((1, per, rows, HEAD), lambda z, k, h: (z, k, 0, 0)),
            ],
            out_specs=pl.BlockSpec((1, per, rows, HEAD), lambda z, k, h: (z, k, 0, 0)),
        ),
        out_shape=jax.ShapeDtypeStruct((Z_SIZE, mats, rows, HEAD), jnp.bfloat16),
        compiler_params=params(),
        name="add_pair",
    )(half, whole, received)


def mix(index, own, received, held, gram, first_row, rows, last):
    mats = own.shape[-3]
    paired = received is not None
    begun = gram is not None

    def body(index_ref, *refs):
        refs = list(refs)
        own_ref = refs.pop(0)
        received_ref = refs.pop(0) if paired else None
        first_ref, second_ref = refs.pop(0), refs.pop(0)
        before_ref = refs.pop(0) if begun else None
        sent_ref, mixed_ref, gram_ref = refs
        k = pl.program_id(0)
        summed = own_ref[...].reshape(rows, HEAD).astype(jnp.float32)
        if paired:
            summed = summed + received_ref[0].astype(jnp.float32)
        rounded = summed.astype(jnp.bfloat16)
        sent_ref[0, 0] = rounded
        summed = rounded.astype(jnp.float32)
        second = index_ref[k] % 2 == 1
        stored = jnp.where(second, second_ref[0].astype(jnp.float32), first_ref[0].astype(jnp.float32))
        renewed = (momentum_rate * stored + summed).astype(jnp.bfloat16)
        mixed = (summed + momentum_rate * renewed.astype(jnp.float32)).astype(jnp.bfloat16)
        mixed_ref[0] = mixed
        part = lax.dot_general(
            mixed, mixed, (((0,), (0,)), ((), ())), preferred_element_type=jnp.float32
        )
        if begun:
            part = part + before_ref[0]
        gram_ref[0] = part.astype(gram_ref.dtype)

    at_row = first_row // rows
    if paired:
        own_spec = pl.BlockSpec((1, 1, rows, HEAD), lambda k, i: (i[mats], k, 0, 0))
    else:
        own_spec = pl.BlockSpec((1, rows, HEAD), lambda k, i: (k, 0, 0))
    in_specs, operands = [own_spec], [own]
    if paired:
        in_specs.append(pl.BlockSpec((1, rows, HEAD), lambda k, i: (k, 0, 0)))
        operands.append(received)
    for one in held:
        in_specs.append(pl.BlockSpec((1, rows, HEAD), lambda k, i: (i[k] // 2, at_row, 0)))
        operands.append(one)
    if begun:
        in_specs.append(pl.BlockSpec((1, HEAD, HEAD), lambda k, i: (k, 0, 0)))
        operands.append(gram)
    return pl.pallas_call(
        body,
        grid_spec=pltpu.PrefetchScalarGridSpec(
            num_scalar_prefetch=1,
            grid=(mats,),
            in_specs=in_specs,
            out_specs=[
                pl.BlockSpec((1, 1, rows, HEAD), lambda k, i: (i[k] // 2, i[k] % 2, 0, 0)),
                pl.BlockSpec((1, rows, HEAD), lambda k, i: (k, 0, 0)),
                pl.BlockSpec((1, HEAD, HEAD), lambda k, i: (k, 0, 0)),
            ],
        ),
        out_shape=[
            jax.ShapeDtypeStruct((held[0].shape[0], 2, rows, HEAD), jnp.bfloat16),
            jax.ShapeDtypeStruct((mats, rows, HEAD), jnp.bfloat16),
            jax.ShapeDtypeStruct((mats, HEAD, HEAD), jnp.bfloat16 if last else jnp.float32),
        ],
        compiler_params=params(),
        name="mix",
    )(index, *operands)


def polynomial(parts):
    count = parts.shape[0]

    def product(a, b):
        return jnp.dot(a, b, preferred_element_type=jnp.float32, precision=lax.Precision.HIGHEST)

    def body(parts_ref, out_ref):
        gram = jnp.sum(parts_ref[...].astype(jnp.float32), axis=0)
        row = lax.broadcasted_iota(jnp.int32, (HEAD, HEAD), 0)
        column = lax.broadcasted_iota(jnp.int32, (HEAD, HEAD), 1)
        unit = jnp.where(row == column, 1.0, 0.0)
        squares = jnp.sum(jnp.sum(gram * unit, axis=0, keepdims=True), axis=1, keepdims=True)
        inverse = 1.0 / (jnp.sqrt(squares) + norm_eps)
        gram = (gram * inverse) * inverse
        turn = None
        for iteration in range(ITERS):
            half = gram.astype(jnp.bfloat16).astype(jnp.float32)
            poly = coef_second * half + coef_third * product(half, half)
            step = coef_first * unit + poly
            if iteration + 1 < ITERS:
                gram = product(step, product(gram, step))
            turn = step if turn is None else product(turn, step)
        turn = turn * (math.sqrt(ROWS) * inverse)
        out_ref[...] = jnp.broadcast_to(turn.astype(jnp.bfloat16)[None], out_ref.shape)

    return pl.pallas_call(
        body,
        out_shape=jax.ShapeDtypeStruct((count, HEAD, HEAD), jnp.bfloat16),
        compiler_params=params(),
        name="polynomial",
    )(parts)


def turn_all(mixed, turns):
    mats = turns.shape[0]
    total = sum(m.shape[1] for m in mixed)

    def body(*refs):
        turn_ref, out_ref = refs[-2], refs[-1]
        at = 0
        for ref in refs[:-2]:
            rows = ref.shape[1]
            out_ref[0, at : at + rows] = jnp.dot(
                ref[0], turn_ref[0], preferred_element_type=jnp.float32
            ).astype(jnp.bfloat16)
            at += rows

    return pl.pallas_call(
        body,
        grid=(mats,),
        in_specs=[pl.BlockSpec((1, m.shape[1], HEAD), lambda k: (k, 0, 0)) for m in mixed]
        + [pl.BlockSpec((1, HEAD, HEAD), lambda k: (k, 0, 0))],
        out_specs=pl.BlockSpec((1, total, HEAD), lambda k: (k, 0, 0)),
        out_shape=jax.ShapeDtypeStruct((mats, total, HEAD), jnp.bfloat16),
        compiler_params=params(),
        name="turn_all",
    )(*mixed, turns)


def renew(filled, stored, arrived):
    slots, sources, total, _ = stored.shape
    per = 4

    def body(filled_ref, stored_ref, *refs):
        out_ref = refs[-1]
        full = filled_ref[pl.program_id(0)] == 1
        at = 0
        for ref in refs[:-1]:
            rows = ref.shape[2]
            here = slice(at, at + rows)
            grad = jnp.where(full, ref[:, 0].astype(jnp.float32), 0.0)
            out_ref[0, :, here] = (
                momentum_rate * stored_ref[0, :, here].astype(jnp.float32) + grad
            ).astype(jnp.bfloat16)
            at += rows

    return pl.pallas_call(
        body,
        grid_spec=pltpu.PrefetchScalarGridSpec(
            num_scalar_prefetch=1,
            grid=(slots, sources // per),
            in_specs=[pl.BlockSpec((1, per, total, HEAD), lambda s, p, f: (s, p, 0, 0))]
            + [
                pl.BlockSpec((per, 1, a.shape[2], HEAD), lambda s, p, f: (p, s, 0, 0))
                for a in arrived
            ],
            out_specs=pl.BlockSpec((1, per, total, HEAD), lambda s, p, f: (s, p, 0, 0)),
        ),
        out_shape=jax.ShapeDtypeStruct(stored.shape, jnp.bfloat16),
        compiler_params=params(),
        name="renew",
    )(filled, stored, *arrived)


def on_device(grads, momentum, owner_table):
    owners = owner_table[0]
    mp_size, slots = owners.shape
    mats = grads.shape[1] // (Z_SIZE * Y_SIZE)
    piece = grads.shape[2]
    me = lax.axis_index("mp")
    half = lax.axis_index("dp") % Y_SIZE
    flat = owners.reshape(-1)
    wanted = jnp.arange(mats, dtype=jnp.int32)
    place = jnp.arange(flat.shape[0], dtype=jnp.int32)
    placed = jnp.sum(jnp.where(flat[None, :] == wanted[:, None], place[None, :], 0), axis=1)
    index = jnp.concatenate([placed, half[None]]).astype(jnp.int32)
    filled = (lax.dynamic_index_in_dim(owners, me, 0, keepdims=False) < mats).astype(jnp.int32)

    own = grads[0].reshape(Z_SIZE, Y_SIZE, mats, piece, HEAD)
    stored = momentum[0, 0].reshape(slots, mp_size, piece, HEAD)

    def chunk(first_row, rows):
        return own[:, :, :, first_row : first_row + rows]

    half_index = half[None].astype(jnp.int32)
    reduced = []
    pending = {}
    for number, (first_row, rows, y_first) in enumerate(CHUNKS):
        if y_first:
            away = lax.dynamic_index_in_dim(chunk(first_row, rows), 1 - half, 1, keepdims=False)
            pending[number] = swap_y(away)
    held = [exchange(stored[s]) for s in range(slots)]
    for number, (first_row, rows, y_first) in enumerate(CHUNKS):
        if y_first:
            paired = add_pair(half_index, own, pending[number], first_row, rows)
            part = scatter_z(paired.reshape(Z_SIZE * mats, rows, HEAD))
            reduced.append((part, None))
        else:
            part = scatter_z(chunk(first_row, rows).reshape(-1, rows, HEAD))
            part = part.reshape(Y_SIZE, mats, rows, HEAD)
            away = lax.dynamic_index_in_dim(part, 1 - half, 0, keepdims=False)
            reduced.append((part, swap_y(away)))

    gram, arrived, mixed = None, [], []
    for number, (first_row, rows, _) in enumerate(CHUNKS):
        part, received = reduced[number]
        last = number + 1 == len(CHUNKS)
        sent, one, gram = mix(index, part, received, held, gram, first_row, rows, last)
        mixed.append(one)
        arrived.append(exchange(sent))
    turns = exchange(polynomial(exchange(gram)))
    update = turn_all(mixed, turns)
    renewed = renew(filled, stored, arrived)
    return (update, renewed.reshape(1, 1, slots, -1, HEAD))


def solution(mesh):
    in_specs = (P("dp", None, "mp", None), P("dp", "mp", None, None, None), P("dp", None, None))
    out_specs = (P("dp", "mp", None), P("dp", "mp", None, None, None))
    return jax.shard_map(
        on_device, mesh=mesh, in_specs=in_specs, out_specs=out_specs, check_vma=False
    )
```

```python
import math

import jax
import jax.numpy as jnp
from jax import lax
from jax.experimental import pallas as pl
from jax.experimental.pallas import tpu as pltpu
from jax.sharding import PartitionSpec as P

ROWS = 8192
HEAD = 128
ITERS = 2

momentum_rate = 0.95
coef_first = 3.4445
coef_second = -4.775
coef_third = 2.0315
norm_eps = 1e-07

Z_SIZE = 4
Y_SIZE = 2
EARLY, PAIRED, LATE = (256, 256), (192, 64), (0, 192)
SOON = (192, 320)
VMEM = 48 * 1024 * 1024


def params():
    return pltpu.CompilerParams(vmem_limit_bytes=VMEM)


def z_groups():
    return [[z * Y_SIZE + y for z in range(Z_SIZE)] for y in range(Y_SIZE)]


def swap_y(x):
    return lax.ppermute(x, "dp", [(i, i ^ 1) for i in range(Z_SIZE * Y_SIZE)])


def scatter_z(x):
    return lax.psum_scatter(
        x, "dp", scatter_dimension=0, tiled=True, axis_index_groups=z_groups()
    )


def barrier(*values):
    return lax.optimization_barrier(values)


def exchange(x):
    return lax.all_to_all(x, "mp", split_axis=0, concat_axis=0, tiled=True)


def shift_z(x, by):
    pairs = [
        (z * Y_SIZE + y, (z + by) % Z_SIZE * Y_SIZE + y) for z in range(Z_SIZE) for y in range(Y_SIZE)
    ]
    return lax.ppermute(x, "dp", pairs)


def whole(*shape):
    return pl.BlockSpec(shape, lambda n, i: (0,) * len(shape))


def add_pair(place, own, received, first_row, rows):
    mats = own.shape[2]

    def body(place_ref, own_ref, received_ref, out_ref):
        out_ref[0] = (
            own_ref[0, 0].astype(jnp.float32) + received_ref[0].astype(jnp.float32)
        ).astype(jnp.bfloat16)

    return pl.pallas_call(
        body,
        grid_spec=pltpu.PrefetchScalarGridSpec(
            num_scalar_prefetch=1,
            grid=(Z_SIZE,),
            in_specs=[
                pl.BlockSpec(
                    (1, 1, mats, rows, HEAD), lambda z, i: (z, i[0], 0, first_row // rows, 0)
                ),
                pl.BlockSpec((1, mats, rows, HEAD), lambda z, i: (z, 0, 0, 0)),
            ],
            out_specs=pl.BlockSpec((1, mats, rows, HEAD), lambda z, i: (z, 0, 0, 0)),
        ),
        out_shape=jax.ShapeDtypeStruct((Z_SIZE, mats, rows, HEAD), jnp.bfloat16),
        compiler_params=params(),
        name="add_pair",
    )(place, own, received)


def mix(index, pieces, held, gram, last):
    mats = index.shape[0] - 2
    owners, piece = held[0].shape[:2]
    begun = gram is not None
    total = sum(rows for _, rows, _ in pieces)
    base = min(first_row for first_row, _, _ in pieces)
    lead = HEAD if last else 0
    terms = [term for _, _, group in pieces for term in group]

    def body(index_ref, *refs):
        refs = list(refs)
        term_refs = [refs.pop(0) for _ in terms]
        held_refs = [refs.pop(0) for _ in held]
        before_ref = refs.pop(0) if begun else None
        sent_ref, mixed_ref = refs[:2]
        for k in range(mats):
            owner, slot = index_ref[2 + k] // 2, index_ref[2 + k] % 2
            part = before_ref[k] if begun else None
            unread = list(zip(term_refs, terms))
            for first_row, rows, group in pieces:
                here, unread = unread[: len(group)], unread[len(group) :]
                summed = sum(
                    (ref[0, k] if isinstance(term, tuple) else ref[k]).astype(jnp.float32)
                    for ref, term in here
                )
                rounded = summed.astype(jnp.bfloat16)
                start = pl.multiple_of(lead + first_row - base + slot * total, 16)
                sent_ref[owner, pl.ds(start, rows)] = rounded
                summed = rounded.astype(jnp.float32)
                first, second = (ref[owner, first_row : first_row + rows] for ref in held_refs)
                stored = jnp.where(slot == 1, second.astype(jnp.float32), first.astype(jnp.float32))
                renewed = (momentum_rate * stored + summed).astype(jnp.bfloat16)
                mixed = (summed + momentum_rate * renewed.astype(jnp.float32)).astype(jnp.bfloat16)
                mixed_ref[k, first_row - base : first_row - base + rows] = mixed
                product = lax.dot_general(
                    mixed, mixed, (((0,), (0,)), ((), ())), preferred_element_type=jnp.float32
                )
                part = product if part is None else part + product
            if last:
                sent_ref[k, :HEAD] = part.astype(jnp.bfloat16)
            else:
                refs[2][k] = part

    in_specs, operands = [], []
    for first_row, rows, group in pieces:
        for term in group:
            if isinstance(term, tuple):
                in_specs.append(
                    pl.BlockSpec((1, mats, rows, HEAD), lambda n, i, at=term[1]: (i[at], 0, 0, 0))
                )
                operands.append(term[0])
            else:
                in_specs.append(whole(mats, rows, HEAD))
                operands.append(term)
    for one in held:
        in_specs.append(whole(owners, piece, HEAD))
        operands.append(one)
    if begun:
        in_specs.append(whole(mats, HEAD, HEAD))
        operands.append(gram)
    shapes = [
        jax.ShapeDtypeStruct((owners, lead + 2 * total, HEAD), jnp.bfloat16),
        jax.ShapeDtypeStruct((mats, total, HEAD), jnp.bfloat16),
    ]
    if not last:
        shapes.append(jax.ShapeDtypeStruct((mats, HEAD, HEAD), jnp.float32))
    return pl.pallas_call(
        body,
        grid_spec=pltpu.PrefetchScalarGridSpec(
            num_scalar_prefetch=1,
            grid=(1,),
            in_specs=in_specs,
            out_specs=[whole(*shape.shape) for shape in shapes],
        ),
        out_shape=shapes,
        compiler_params=params(),
        name="mix",
    )(index, *operands)


def polynomial(parts):
    count = parts.shape[0]

    def product(a, b):
        return jnp.dot(a, b, preferred_element_type=jnp.float32, precision=lax.Precision.HIGHEST)

    def body(parts_ref, out_ref):
        gram = jnp.sum(parts_ref[...].astype(jnp.float32), axis=0)
        row = lax.broadcasted_iota(jnp.int32, (HEAD, HEAD), 0)
        column = lax.broadcasted_iota(jnp.int32, (HEAD, HEAD), 1)
        unit = jnp.where(row == column, 1.0, 0.0)
        squares = jnp.sum(jnp.sum(gram * unit, axis=0, keepdims=True), axis=1, keepdims=True)
        inverse = 1.0 / (jnp.sqrt(squares) + norm_eps)
        gram = (gram * inverse) * inverse
        turn = None
        for iteration in range(ITERS):
            half = gram.astype(jnp.bfloat16).astype(jnp.float32)
            poly = coef_second * half + coef_third * product(half, half)
            step = coef_first * unit + poly
            if iteration + 1 < ITERS:
                gram = product(step, product(gram, step))
            turn = step if turn is None else product(turn, step)
        turn = turn * (math.sqrt(ROWS) * inverse)
        out_ref[...] = jnp.broadcast_to(turn.astype(jnp.bfloat16)[None], out_ref.shape)

    return pl.pallas_call(
        body,
        grid=(1,),
        in_specs=[pl.BlockSpec((count, HEAD, HEAD), lambda n: (0, 0, 0))],
        out_specs=pl.BlockSpec((count, HEAD, HEAD), lambda n: (0, 0, 0)),
        out_shape=jax.ShapeDtypeStruct((count, HEAD, HEAD), jnp.bfloat16),
        compiler_params=params(),
        name="polynomial",
    )(parts)


def turn_all(late, soon, turns):
    mats = turns.shape[0]
    piece = LATE[1] + SOON[1]
    per = 2

    def body(late_ref, soon_ref, turn_ref, out_ref):
        for k in range(per):
            for ref, (first_row, rows) in ((late_ref, LATE), (soon_ref, SOON)):
                out_ref[k, first_row : first_row + rows] = jnp.dot(
                    ref[k], turn_ref[k], preferred_element_type=jnp.float32
                ).astype(jnp.bfloat16)

    def block(rows):
        return pl.BlockSpec((per, rows, HEAD), lambda k: (k, 0, 0))

    return pl.pallas_call(
        body,
        grid=(mats // per,),
        in_specs=[block(LATE[1]), block(SOON[1]), block(HEAD)],
        out_specs=block(piece),
        out_shape=jax.ShapeDtypeStruct((mats, piece, HEAD), jnp.bfloat16),
        compiler_params=params(),
        name="turn_all",
    )(late, soon, turns)


def renew(filled, stored, arrived, done, first_row, rows):
    slots, sources, _, _ = stored.shape
    lead = arrived.shape[1] - slots * rows
    unit = math.gcd(first_row, rows)
    per = 8

    def body(filled_ref, stored_ref, arrived_ref, *refs):
        out_ref = refs[-1]
        at = pl.program_id(1) * unit
        for slot in range(slots):
            start = pl.multiple_of(lead + slot * rows + at, 16)
            grad = arrived_ref[:, pl.ds(start, unit)].astype(jnp.float32)
            grad = jnp.where(filled_ref[slot] == 1, grad, 0.0)
            out_ref[slot] = (
                momentum_rate * stored_ref[slot].astype(jnp.float32) + grad
            ).astype(jnp.bfloat16)

    here = pl.BlockSpec((slots, per, unit, HEAD), lambda p, r, f: (0, p, first_row // unit + r, 0))
    return pl.pallas_call(
        body,
        grid_spec=pltpu.PrefetchScalarGridSpec(
            num_scalar_prefetch=1,
            grid=(sources // per, rows // unit),
            in_specs=[here, pl.BlockSpec((per, lead + slots * rows, HEAD), lambda p, r, f: (p, 0, 0))]
            + [pl.BlockSpec(memory_space=pl.ANY)] * (done is not None),
            out_specs=here,
        ),
        out_shape=jax.ShapeDtypeStruct(stored.shape, jnp.bfloat16),
        input_output_aliases={3: 0} if done is not None else {},
        compiler_params=params(),
        name="renew",
    )(filled, stored, arrived, *([done] if done is not None else []))


def on_device(grads, momentum, owner_table):
    owners = owner_table[0]
    mp_size, slots = owners.shape
    mats = grads.shape[1] // (Z_SIZE * Y_SIZE)
    piece = grads.shape[2]
    me = lax.axis_index("mp")
    place = lax.axis_index("dp")
    level, half = place // Y_SIZE, place % Y_SIZE
    flat = owners.reshape(-1)
    wanted = jnp.arange(mats, dtype=jnp.int32)
    position = jnp.arange(flat.shape[0], dtype=jnp.int32)
    placed = jnp.sum(jnp.where(flat[None, :] == wanted[:, None], position[None, :], 0), axis=1)
    place = jnp.stack([half, level]).astype(jnp.int32)
    index = jnp.concatenate([place, placed.astype(jnp.int32)])
    filled = (lax.dynamic_index_in_dim(owners, me, 0, keepdims=False) < mats).astype(jnp.int32)

    own = grads[0].reshape(Z_SIZE, Y_SIZE, mats, piece, HEAD)
    stored = momentum[0, 0].reshape(slots, mp_size, piece, HEAD)

    def half_away(part):
        return lax.dynamic_index_in_dim(part, 1 - half, 0, keepdims=False)

    def rows_of(array, chunk):
        first_row, rows = chunk
        return array[:, :, :, first_row : first_row + rows]

    away, own1 = barrier(
        lax.dynamic_index_in_dim(rows_of(own, PAIRED), 1 - half, 1, keepdims=False), own
    )
    early, own2 = barrier(rows_of(own1, EARLY), own1)
    late = rows_of(own2, LATE)
    early, late = (
        scatter_z(part.reshape(-1, part.shape[3], HEAD)).reshape(Y_SIZE, mats, -1, HEAD)
        for part in (early, late)
    )
    received, later = barrier(swap_y(away), stored[1])
    paired, later = barrier(add_pair(place, own, received, *PAIRED), later)
    held = [exchange(stored[0]), exchange(later)]
    shifted = [
        shift_z(lax.dynamic_index_in_dim(paired, (level + by) % Z_SIZE, 0, keepdims=False), by)
        for by in range(1, Z_SIZE)
    ]
    sent, mixed_soon, gram = mix(
        index,
        [
            (*EARLY, [(early, 0), swap_y(half_away(early))]),
            (*PAIRED, [(paired, 1), *shifted]),
        ],
        held,
        None,
        False,
    )
    late, _ = barrier(late, sent)
    renewed = renew(filled, stored, exchange(sent), None, *SOON)
    renewed, received = barrier(renewed, swap_y(half_away(late)))
    sent, mixed_late = mix(index, [(*LATE, [(late, 0), received])], held, gram, True)
    arrived = exchange(sent)
    turns = exchange(polynomial(arrived))
    renewed = renew(filled, stored, arrived, renewed, *LATE)
    update = turn_all(mixed_late, mixed_soon, turns)
    return (update, renewed.reshape(1, 1, slots, -1, HEAD))


def solution(mesh):
    in_specs = (P("dp", None, "mp", None), P("dp", "mp", None, None, None), P("dp", None, None))
    out_specs = (P("dp", "mp", None), P("dp", "mp", None, None, None))
    return jax.shard_map(
        on_device, mesh=mesh, in_specs=in_specs, out_specs=out_specs, check_vma=False
    )
```

```python
import math

import jax
import jax.numpy as jnp
from jax import lax
from jax.experimental import pallas as pl
from jax.experimental.pallas import tpu as pltpu
from jax.sharding import PartitionSpec as P

ROWS = 8192
HEAD = 128
ITERS = 2

momentum_rate = 0.95
coef_first = 3.4445
coef_second = -4.775
coef_third = 2.0315
norm_eps = 1e-07

Z_SIZE = 4
Y_SIZE = 2
PAIRED, LATE, EARLY = (0, 64), (64, 176), (240, 272)
LAST = (0, 240)
VMEM = 48 * 1024 * 1024


def params():
    return pltpu.CompilerParams(vmem_limit_bytes=VMEM)


def z_groups():
    return [[z * Y_SIZE + y for z in range(Z_SIZE)] for y in range(Y_SIZE)]


def swap_y(x):
    return lax.ppermute(x, "dp", [(i, i ^ 1) for i in range(Z_SIZE * Y_SIZE)])


def scatter_z(x):
    return lax.psum_scatter(
        x, "dp", scatter_dimension=0, tiled=True, axis_index_groups=z_groups()
    )


def barrier(*values):
    return lax.optimization_barrier(values)


def exchange(x):
    return lax.all_to_all(x, "mp", split_axis=0, concat_axis=0, tiled=True)


def shift_z(x, by):
    pairs = [
        (z * Y_SIZE + y, (z + by) % Z_SIZE * Y_SIZE + y) for z in range(Z_SIZE) for y in range(Y_SIZE)
    ]
    return lax.ppermute(x, "dp", pairs)


def whole(*shape):
    return pl.BlockSpec(shape, lambda n, i: (0,) * len(shape))


def copy_rows(place, own, chunk, blocks, steps, at):
    first_row, rows = chunk
    mats = own.shape[2]

    def body(place_ref, *refs):
        for source, target in zip(refs[:blocks], refs[blocks:]):
            target[...] = source[0]

    return pl.pallas_call(
        body,
        grid_spec=pltpu.PrefetchScalarGridSpec(
            num_scalar_prefetch=1,
            grid=(steps,),
            in_specs=[
                pl.BlockSpec(
                    (1, 1, mats, rows, HEAD),
                    lambda n, i, block=block: (*at(block, n, i), 0, first_row // rows, 0),
                )
                for block in range(blocks)
            ],
            out_specs=[pl.BlockSpec((1, mats, rows, HEAD), lambda n, i: (n, 0, 0, 0))] * blocks,
        ),
        out_shape=[jax.ShapeDtypeStruct((steps, mats, rows, HEAD), jnp.bfloat16)] * blocks,
        compiler_params=params(),
        name="copy_rows",
    )(place, *[own] * blocks)


def add_pair(place, own, received, first_row, rows):
    mats = own.shape[2]

    def body(place_ref, own_ref, received_ref, out_ref):
        out_ref[0] = (
            own_ref[0, 0].astype(jnp.float32) + received_ref[0].astype(jnp.float32)
        ).astype(jnp.bfloat16)

    return pl.pallas_call(
        body,
        grid_spec=pltpu.PrefetchScalarGridSpec(
            num_scalar_prefetch=1,
            grid=(Z_SIZE,),
            in_specs=[
                pl.BlockSpec(
                    (1, 1, mats, rows, HEAD), lambda z, i: (z, i[0], 0, first_row // rows, 0)
                ),
                pl.BlockSpec((1, mats, rows, HEAD), lambda z, i: (z, 0, 0, 0)),
            ],
            out_specs=pl.BlockSpec((1, mats, rows, HEAD), lambda z, i: (z, 0, 0, 0)),
        ),
        out_shape=jax.ShapeDtypeStruct((Z_SIZE, mats, rows, HEAD), jnp.bfloat16),
        compiler_params=params(),
        name="add_pair",
    )(place, own, received)


def mix(index, pieces, held, gram, last):
    mats = index.shape[0] - 2
    owners = held.shape[0]
    begun = gram is not None
    total = sum(rows for _, rows, _ in pieces)
    base = min(first_row for first_row, _, _ in pieces)
    lead = HEAD if last else 0
    terms = [term for _, _, group in pieces for term in group]

    def body(index_ref, *refs):
        refs = list(refs)
        term_refs = [refs.pop(0) for _ in terms]
        held_ref = refs.pop(0)
        before_ref = refs.pop(0) if begun else None
        sent_ref, mixed_ref = refs[:2]
        for k in range(mats):
            owner, slot = index_ref[2 + k] // 2, index_ref[2 + k] % 2
            part = before_ref[k] if begun else None
            unread = list(term_refs)
            for first_row, rows, group in pieces:
                here, unread = unread[: len(group)], unread[len(group) :]
                summed = sum(
                    ref[(0,) * (len(ref.shape) - 3) + (k,)].astype(jnp.float32)
                    for ref in here
                )
                rounded = summed.astype(jnp.bfloat16)
                start = pl.multiple_of(lead + first_row - base + slot * total, 16)
                sent_ref[owner, pl.ds(start, rows)] = rounded
                summed = rounded.astype(jnp.float32)
                stored = held_ref[owner, slot, first_row : first_row + rows].astype(jnp.float32)
                renewed = (momentum_rate * stored + summed).astype(jnp.bfloat16)
                mixed = (summed + momentum_rate * renewed.astype(jnp.float32)).astype(jnp.bfloat16)
                mixed_ref[k, first_row - base : first_row - base + rows] = mixed
                product = lax.dot_general(
                    mixed, mixed, (((0,), (0,)), ((), ())), preferred_element_type=jnp.float32
                )
                part = product if part is None else part + product
            if last:
                sent_ref[k, :HEAD] = part.astype(jnp.bfloat16)
            else:
                refs[2][k] = part

    in_specs, operands = [], []
    for first_row, rows, group in pieces:
        for term in group:
            if isinstance(term, tuple):
                in_specs.append(
                    pl.BlockSpec((1,) * (term[0].ndim - 3) + (mats, rows, HEAD), term[1])
                )
                operands.append(term[0])
            else:
                in_specs.append(whole(mats, rows, HEAD))
                operands.append(term)
    in_specs.append(whole(*held.shape))
    operands.append(held)
    if begun:
        in_specs.append(whole(mats, HEAD, HEAD))
        operands.append(gram)
    shapes = [
        jax.ShapeDtypeStruct((owners, lead + 2 * total, HEAD), jnp.bfloat16),
        jax.ShapeDtypeStruct((mats, total, HEAD), jnp.bfloat16),
    ]
    if not last:
        shapes.append(jax.ShapeDtypeStruct((mats, HEAD, HEAD), jnp.float32))
    return pl.pallas_call(
        body,
        grid_spec=pltpu.PrefetchScalarGridSpec(
            num_scalar_prefetch=1,
            grid=(1,),
            in_specs=in_specs,
            out_specs=[whole(*shape.shape) for shape in shapes],
        ),
        out_shape=shapes,
        compiler_params=params(),
        name="mix",
    )(index, *operands)


def polynomial(parts):
    count = parts.shape[0]

    def product(a, b):
        return jnp.dot(a, b, preferred_element_type=jnp.float32, precision=lax.Precision.HIGHEST)

    def body(parts_ref, out_ref):
        gram = jnp.sum(parts_ref[...].astype(jnp.float32), axis=0)
        row = lax.broadcasted_iota(jnp.int32, (HEAD, HEAD), 0)
        column = lax.broadcasted_iota(jnp.int32, (HEAD, HEAD), 1)
        unit = jnp.where(row == column, 1.0, 0.0)
        squares = jnp.sum(jnp.sum(gram * unit, axis=0, keepdims=True), axis=1, keepdims=True)
        inverse = 1.0 / (jnp.sqrt(squares) + norm_eps)
        gram = (gram * inverse) * inverse
        turn = None
        for iteration in range(ITERS):
            half = gram.astype(jnp.bfloat16).astype(jnp.float32)
            poly = coef_second * half + coef_third * product(half, half)
            step = coef_first * unit + poly
            if iteration + 1 < ITERS:
                gram = product(step, product(gram, step))
            turn = step if turn is None else product(turn, step)
        turn = turn * (math.sqrt(ROWS) * inverse)
        out_ref[...] = jnp.broadcast_to(turn.astype(jnp.bfloat16)[None], out_ref.shape)

    return pl.pallas_call(
        body,
        grid=(1,),
        in_specs=[pl.BlockSpec((count, HEAD, HEAD), lambda n: (0, 0, 0))],
        out_specs=pl.BlockSpec((count, HEAD, HEAD), lambda n: (0, 0, 0)),
        out_shape=jax.ShapeDtypeStruct((count, HEAD, HEAD), jnp.bfloat16),
        compiler_params=params(),
        name="polynomial",
    )(parts)


def turn_all(last, early, turns):
    mats = turns.shape[0]
    piece = LAST[1] + EARLY[1]
    per = 2

    def body(last_ref, early_ref, turn_ref, out_ref):
        for k in range(per):
            for ref, (first_row, rows) in ((last_ref, LAST), (early_ref, EARLY)):
                out_ref[k, first_row : first_row + rows] = jnp.dot(
                    ref[k], turn_ref[k], preferred_element_type=jnp.float32
                ).astype(jnp.bfloat16)

    def block(rows):
        return pl.BlockSpec((per, rows, HEAD), lambda k: (k, 0, 0))

    return pl.pallas_call(
        body,
        grid=(mats // per,),
        in_specs=[block(LAST[1]), block(EARLY[1]), block(HEAD)],
        out_specs=block(piece),
        out_shape=jax.ShapeDtypeStruct((mats, piece, HEAD), jnp.bfloat16),
        compiler_params=params(),
        name="turn_all",
    )(last, early, turns)


def renew(filled, stored, arrived, done, first_row, rows):
    slots, sources, _, _ = stored.shape
    lead = arrived.shape[1] - slots * rows
    piece = rows if first_row % rows == 0 else stored.shape[2]
    at = 0 if first_row % rows == 0 else first_row
    per = 4

    def body(filled_ref, stored_ref, arrived_ref, *refs):
        out_ref = refs[-1]
        here = slice(at, at + rows)
        for slot in range(slots):
            start = lead + slot * rows
            grad = arrived_ref[:, start : start + rows].astype(jnp.float32)
            grad = jnp.where(filled_ref[slot] == 1, grad, 0.0)
            out_ref[slot, :, here] = (
                momentum_rate * stored_ref[slot, :, here].astype(jnp.float32) + grad
            ).astype(jnp.bfloat16)

    block = pl.BlockSpec((slots, per, piece, HEAD), lambda p, f: (0, p, first_row // piece, 0))
    return pl.pallas_call(
        body,
        grid_spec=pltpu.PrefetchScalarGridSpec(
            num_scalar_prefetch=1,
            grid=(sources // per,),
            in_specs=[block, pl.BlockSpec((per, lead + slots * rows, HEAD), lambda p, f: (p, 0, 0))]
            + [pl.BlockSpec(memory_space=pl.ANY)] * (done is not None),
            out_specs=block,
        ),
        out_shape=jax.ShapeDtypeStruct(stored.shape, jnp.bfloat16),
        input_output_aliases={3: 0} if done is not None else {},
        compiler_params=params(),
        name="renew",
    )(filled, stored, arrived, *([done] if done is not None else []))


def on_device(grads, momentum, owner_table):
    owners = owner_table[0]
    mp_size, slots = owners.shape
    mats = grads.shape[1] // (Z_SIZE * Y_SIZE)
    piece = grads.shape[2]
    me = lax.axis_index("mp")
    place = lax.axis_index("dp")
    level, half = place // Y_SIZE, place % Y_SIZE
    flat = owners.reshape(-1)
    wanted = jnp.arange(mats, dtype=jnp.int32)
    position = jnp.arange(flat.shape[0], dtype=jnp.int32)
    placed = jnp.sum(jnp.where(flat[None, :] == wanted[:, None], position[None, :], 0), axis=1)
    place = jnp.stack([half, level]).astype(jnp.int32)
    index = jnp.concatenate([place, placed.astype(jnp.int32)])
    filled = (lax.dynamic_index_in_dim(owners, me, 0, keepdims=False) < mats).astype(jnp.int32)

    own = grads[0].reshape(Z_SIZE, Y_SIZE, mats, piece, HEAD)
    stored = momentum[0, 0].reshape(slots, mp_size, piece, HEAD)

    def half_away(part):
        return lax.dynamic_index_in_dim(part, 1 - half, 0, keepdims=False)

    def own_half(n, i):
        return (i[0], 0, 0, 0)

    def own_level(n, i):
        return (i[1], 0, 0, 0)

    def half_away(part):
        return lax.dynamic_index_in_dim(part, 1 - half, 0, keepdims=False)

    early, own1 = barrier(own[:, :, :, EARLY[0] : EARLY[0] + EARLY[1]], own)
    early = scatter_z(early.reshape(-1, EARLY[1], HEAD)).reshape(Y_SIZE, mats, -1, HEAD)
    (away,) = copy_rows(place, own1, PAIRED, 1, Z_SIZE, lambda block, n, i: (n, 1 - i[0]))
    away, turned = barrier(away, stored.swapaxes(0, 1))
    turned, own2 = barrier(turned, own1)
    received = swap_y(away)
    held, own2 = barrier(exchange(turned), own2)
    late = own2[:, :, :, LATE[0] : LATE[0] + LATE[1]].reshape(-1, LATE[1], HEAD)
    late = scatter_z(late).reshape(Y_SIZE, mats, -1, HEAD)
    early, held, received = barrier(early, held, received)
    early_away = swap_y(half_away(early))
    paired = add_pair(place, own, received, *PAIRED)
    shifted = [
        shift_z(lax.dynamic_index_in_dim(paired, (level + by) % Z_SIZE, 0, keepdims=False), by)
        for by in range(1, Z_SIZE)
    ]
    pieces = [(*EARLY, [(early, own_half), early_away])]
    sent, mixed_early, gram = mix(index, pieces, held, None, False)
    late, _ = barrier(late, sent)
    renewed = renew(filled, stored, exchange(sent), None, *EARLY)
    renewed, received = barrier(renewed, swap_y(half_away(late)))
    pieces = [
        (*PAIRED, [(paired, own_level), *shifted]),
        (*LATE, [(late, own_half), received]),
    ]
    sent, mixed_last = mix(index, pieces, held, gram, True)
    arrived = exchange(sent)
    turns = exchange(polynomial(arrived))
    renewed = renew(filled, stored, arrived, renewed, *LAST)
    update = turn_all(mixed_last, mixed_early, turns)
    return (update, renewed.reshape(1, 1, slots, -1, HEAD))


def solution(mesh):
    in_specs = (P("dp", None, "mp", None), P("dp", "mp", None, None, None), P("dp", None, None))
    out_specs = (P("dp", "mp", None), P("dp", "mp", None, None, None))
    return jax.shard_map(
        on_device, mesh=mesh, in_specs=in_specs, out_specs=out_specs, check_vma=False
    )
```

```python
import math

import jax
import jax.numpy as jnp
from jax import lax
from jax.experimental import pallas as pl
from jax.experimental.pallas import tpu as pltpu
from jax.sharding import PartitionSpec as P

ROWS = 8192
HEAD = 128
ITERS = 2

momentum_rate = 0.95
coef_first = 3.4445
coef_second = -4.775
coef_third = 2.0315
norm_eps = 1e-07

Z_SIZE = 4
Y_SIZE = 2
PAIRED, LATE, EARLY = (0, 64), (64, 176), (240, 272)
LAST = (0, 240)
VMEM = 48 * 1024 * 1024
MOST_VMEM = 60 * 1024 * 1024


def params(limit=VMEM):
    return pltpu.CompilerParams(vmem_limit_bytes=limit)


def z_groups():
    return [[z * Y_SIZE + y for z in range(Z_SIZE)] for y in range(Y_SIZE)]


def swap_y(x):
    return lax.ppermute(x, "dp", [(i, i ^ 1) for i in range(Z_SIZE * Y_SIZE)])


def scatter_z(x):
    return lax.psum_scatter(
        x, "dp", scatter_dimension=0, tiled=True, axis_index_groups=z_groups()
    )


def barrier(*values):
    return lax.optimization_barrier(values)


def exchange(x):
    return lax.all_to_all(x, "mp", split_axis=0, concat_axis=0, tiled=True)


def shift_z(x, by):
    pairs = [
        (z * Y_SIZE + y, (z + by) % Z_SIZE * Y_SIZE + y) for z in range(Z_SIZE) for y in range(Y_SIZE)
    ]
    return lax.ppermute(x, "dp", pairs)


def whole(*shape):
    return pl.BlockSpec(shape, lambda n, i: (0,) * len(shape))


def copy_rows(place, own, chunk, blocks, steps, at):
    first_row, rows = chunk
    mats = own.shape[2]

    def body(place_ref, *refs):
        for source, target in zip(refs[:blocks], refs[blocks:]):
            target[...] = source[0]

    return pl.pallas_call(
        body,
        grid_spec=pltpu.PrefetchScalarGridSpec(
            num_scalar_prefetch=1,
            grid=(steps,),
            in_specs=[
                pl.BlockSpec(
                    (1, 1, mats, rows, HEAD),
                    lambda n, i, block=block: (*at(block, n, i), 0, first_row // rows, 0),
                )
                for block in range(blocks)
            ],
            out_specs=[pl.BlockSpec((1, mats, rows, HEAD), lambda n, i: (n, 0, 0, 0))] * blocks,
        ),
        out_shape=[jax.ShapeDtypeStruct((steps, mats, rows, HEAD), jnp.bfloat16)] * blocks,
        compiler_params=params(),
        name="copy_rows",
    )(place, *[own] * blocks)


def add_pair(place, own, received, first_row, rows):
    mats = own.shape[2]

    def body(place_ref, own_ref, received_ref, out_ref):
        out_ref[0] = (
            own_ref[0, 0].astype(jnp.float32) + received_ref[0].astype(jnp.float32)
        ).astype(jnp.bfloat16)

    return pl.pallas_call(
        body,
        grid_spec=pltpu.PrefetchScalarGridSpec(
            num_scalar_prefetch=1,
            grid=(Z_SIZE,),
            in_specs=[
                pl.BlockSpec(
                    (1, 1, mats, rows, HEAD), lambda z, i: (z, i[0], 0, first_row // rows, 0)
                ),
                pl.BlockSpec((1, mats, rows, HEAD), lambda z, i: (z, 0, 0, 0)),
            ],
            out_specs=pl.BlockSpec((1, mats, rows, HEAD), lambda z, i: (z, 0, 0, 0)),
        ),
        out_shape=jax.ShapeDtypeStruct((Z_SIZE, mats, rows, HEAD), jnp.bfloat16),
        compiler_params=params(),
        name="add_pair",
    )(place, own, received)


def mix(index, pieces, held, gram, last):
    mats = index.shape[0] - 2
    owners = held.shape[0]
    begun = gram is not None
    total = sum(rows for _, rows, _ in pieces)
    base = min(first_row for first_row, _, _ in pieces)
    lead = HEAD if last else 0
    terms = [term for _, _, group in pieces for term in group]

    def body(index_ref, *refs):
        refs = list(refs)
        term_refs = [refs.pop(0) for _ in terms]
        held_ref = refs.pop(0)
        before_ref = refs.pop(0) if begun else None
        sent_ref, mixed_ref = refs[:2]
        for k in range(mats):
            owner, slot = index_ref[2 + k] // 2, index_ref[2 + k] % 2
            part = before_ref[k] if begun else None
            unread = list(term_refs)
            for first_row, rows, group in pieces:
                here, unread = unread[: len(group)], unread[len(group) :]
                summed = sum(
                    ref[(0,) * (len(ref.shape) - 3) + (k,)].astype(jnp.float32)
                    for ref in here
                )
                rounded = summed.astype(jnp.bfloat16)
                start = pl.multiple_of(lead + first_row - base + slot * total, 16)
                sent_ref[owner, pl.ds(start, rows)] = rounded
                summed = rounded.astype(jnp.float32)
                stored = held_ref[owner, slot, first_row : first_row + rows].astype(jnp.float32)
                renewed = (momentum_rate * stored + summed).astype(jnp.bfloat16)
                mixed = (summed + momentum_rate * renewed.astype(jnp.float32)).astype(jnp.bfloat16)
                mixed_ref[k, first_row - base : first_row - base + rows] = mixed
                product = lax.dot_general(
                    mixed, mixed, (((0,), (0,)), ((), ())), preferred_element_type=jnp.float32
                )
                part = product if part is None else part + product
            if last:
                sent_ref[k, :HEAD] = part.astype(jnp.bfloat16)
            else:
                refs[2][k] = part

    in_specs, operands = [], []
    for first_row, rows, group in pieces:
        for term in group:
            if isinstance(term, tuple):
                in_specs.append(
                    pl.BlockSpec((1,) * (term[0].ndim - 3) + (mats, rows, HEAD), term[1])
                )
                operands.append(term[0])
            else:
                in_specs.append(whole(mats, rows, HEAD))
                operands.append(term)
    in_specs.append(whole(*held.shape))
    operands.append(held)
    if begun:
        in_specs.append(whole(mats, HEAD, HEAD))
        operands.append(gram)
    shapes = [
        jax.ShapeDtypeStruct((owners, lead + 2 * total, HEAD), jnp.bfloat16),
        jax.ShapeDtypeStruct((mats, total, HEAD), jnp.bfloat16),
    ]
    if not last:
        shapes.append(jax.ShapeDtypeStruct((mats, HEAD, HEAD), jnp.float32))
    return pl.pallas_call(
        body,
        grid_spec=pltpu.PrefetchScalarGridSpec(
            num_scalar_prefetch=1,
            grid=(1,),
            in_specs=in_specs,
            out_specs=[whole(*shape.shape) for shape in shapes],
        ),
        out_shape=shapes,
        compiler_params=params(VMEM if last else MOST_VMEM),
        name="mix",
    )(index, *operands)


def polynomial(parts):
    count = parts.shape[0]

    def product(a, b):
        return jnp.dot(a, b, preferred_element_type=jnp.float32, precision=lax.Precision.HIGHEST)

    def body(parts_ref, out_ref):
        gram = jnp.sum(parts_ref[...].astype(jnp.float32), axis=0)
        row = lax.broadcasted_iota(jnp.int32, (HEAD, HEAD), 0)
        column = lax.broadcasted_iota(jnp.int32, (HEAD, HEAD), 1)
        unit = jnp.where(row == column, 1.0, 0.0)
        squares = jnp.sum(jnp.sum(gram * unit, axis=0, keepdims=True), axis=1, keepdims=True)
        inverse = 1.0 / (jnp.sqrt(squares) + norm_eps)
        gram = (gram * inverse) * inverse
        turn = None
        for iteration in range(ITERS):
            half = gram.astype(jnp.bfloat16).astype(jnp.float32)
            poly = coef_second * half + coef_third * product(half, half)
            step = coef_first * unit + poly
            if iteration + 1 < ITERS:
                gram = product(step, product(gram, step))
            turn = step if turn is None else product(turn, step)
        turn = turn * (math.sqrt(ROWS) * inverse)
        out_ref[...] = jnp.broadcast_to(turn.astype(jnp.bfloat16)[None], out_ref.shape)

    return pl.pallas_call(
        body,
        grid=(1,),
        in_specs=[pl.BlockSpec((count, HEAD, HEAD), lambda n: (0, 0, 0))],
        out_specs=pl.BlockSpec((count, HEAD, HEAD), lambda n: (0, 0, 0)),
        out_shape=jax.ShapeDtypeStruct((count, HEAD, HEAD), jnp.bfloat16),
        compiler_params=params(),
        name="polynomial",
    )(parts)


def turn_all(last, early, turns):
    mats = turns.shape[0]
    piece = LAST[1] + EARLY[1]
    per = 2

    def body(last_ref, early_ref, turn_ref, out_ref):
        for k in range(per):
            for ref, (first_row, rows) in ((last_ref, LAST), (early_ref, EARLY)):
                out_ref[k, first_row : first_row + rows] = jnp.dot(
                    ref[k], turn_ref[k], preferred_element_type=jnp.float32
                ).astype(jnp.bfloat16)

    def block(rows):
        return pl.BlockSpec((per, rows, HEAD), lambda k: (k, 0, 0))

    return pl.pallas_call(
        body,
        grid=(mats // per,),
        in_specs=[block(LAST[1]), block(EARLY[1]), block(HEAD)],
        out_specs=block(piece),
        out_shape=jax.ShapeDtypeStruct((mats, piece, HEAD), jnp.bfloat16),
        compiler_params=params(),
        name="turn_all",
    )(last, early, turns)


def renew(filled, stored, arrived, done, first_row, rows):
    slots, sources, _, _ = stored.shape
    lead = arrived.shape[1] - slots * rows
    piece = rows if first_row % rows == 0 else stored.shape[2]
    at = 0 if first_row % rows == 0 else first_row
    per = 4

    def body(filled_ref, stored_ref, arrived_ref, *refs):
        out_ref = refs[-1]
        here = slice(at, at + rows)
        for slot in range(slots):
            start = lead + slot * rows
            grad = arrived_ref[:, start : start + rows].astype(jnp.float32)
            grad = jnp.where(filled_ref[slot] == 1, grad, 0.0)
            out_ref[slot, :, here] = (
                momentum_rate * stored_ref[slot, :, here].astype(jnp.float32) + grad
            ).astype(jnp.bfloat16)

    block = pl.BlockSpec((slots, per, piece, HEAD), lambda p, f: (0, p, first_row // piece, 0))
    return pl.pallas_call(
        body,
        grid_spec=pltpu.PrefetchScalarGridSpec(
            num_scalar_prefetch=1,
            grid=(sources // per,),
            in_specs=[block, pl.BlockSpec((per, lead + slots * rows, HEAD), lambda p, f: (p, 0, 0))]
            + [pl.BlockSpec(memory_space=pl.ANY)] * (done is not None),
            out_specs=block,
        ),
        out_shape=jax.ShapeDtypeStruct(stored.shape, jnp.bfloat16),
        input_output_aliases={3: 0} if done is not None else {},
        compiler_params=params(),
        name="renew",
    )(filled, stored, arrived, *([done] if done is not None else []))


def on_device(grads, momentum, owner_table):
    owners = owner_table[0]
    mp_size, slots = owners.shape
    mats = grads.shape[1] // (Z_SIZE * Y_SIZE)
    piece = grads.shape[2]
    me = lax.axis_index("mp")
    place = lax.axis_index("dp")
    level, half = place // Y_SIZE, place % Y_SIZE
    flat = owners.reshape(-1)
    wanted = jnp.arange(mats, dtype=jnp.int32)
    position = jnp.arange(flat.shape[0], dtype=jnp.int32)
    placed = jnp.sum(jnp.where(flat[None, :] == wanted[:, None], position[None, :], 0), axis=1)
    place = jnp.stack([half, level]).astype(jnp.int32)
    index = jnp.concatenate([place, placed.astype(jnp.int32)])
    filled = (lax.dynamic_index_in_dim(owners, me, 0, keepdims=False) < mats).astype(jnp.int32)

    own = grads[0].reshape(Z_SIZE, Y_SIZE, mats, piece, HEAD)
    stored = momentum[0, 0].reshape(slots, mp_size, piece, HEAD)

    def half_away(part):
        return lax.dynamic_index_in_dim(part, 1 - half, 0, keepdims=False)

    def own_half(n, i):
        return (i[0], 0, 0, 0)

    def own_level(n, i):
        return (i[1], 0, 0, 0)

    def half_away(part):
        return lax.dynamic_index_in_dim(part, 1 - half, 0, keepdims=False)

    early, own1 = barrier(own[:, :, :, EARLY[0] : EARLY[0] + EARLY[1]], own)
    early = scatter_z(early.reshape(-1, EARLY[1], HEAD)).reshape(Y_SIZE, mats, -1, HEAD)
    (away,) = copy_rows(place, own1, PAIRED, 1, Z_SIZE, lambda block, n, i: (n, 1 - i[0]))
    away, turned = barrier(away, stored.swapaxes(0, 1))
    turned, own2 = barrier(turned, own1)
    received = swap_y(away)
    held, own2 = barrier(exchange(turned), own2)
    late = own2[:, :, :, LATE[0] : LATE[0] + LATE[1]].reshape(-1, LATE[1], HEAD)
    late = scatter_z(late).reshape(Y_SIZE, mats, -1, HEAD)
    early, held, received = barrier(early, held, received)
    early_away = swap_y(half_away(early))
    paired = add_pair(place, own, received, *PAIRED)
    shifted = [
        shift_z(lax.dynamic_index_in_dim(paired, (level + by) % Z_SIZE, 0, keepdims=False), by)
        for by in range(1, Z_SIZE)
    ]
    pieces = [(*EARLY, [(early, own_half), early_away])]
    sent, mixed_early, gram = mix(index, pieces, held, None, False)
    late, _ = barrier(late, sent)
    renewed = renew(filled, stored, exchange(sent), None, *EARLY)
    renewed, received = barrier(renewed, swap_y(half_away(late)))
    pieces = [
        (*PAIRED, [(paired, own_level), *shifted]),
        (*LATE, [(late, own_half), received]),
    ]
    sent, mixed_last = mix(index, pieces, held, gram, True)
    arrived = exchange(sent)
    turns = exchange(polynomial(arrived))
    renewed = renew(filled, stored, arrived, renewed, *LAST)
    update = turn_all(mixed_last, mixed_early, turns)
    return (update, renewed.reshape(1, 1, slots, -1, HEAD))


def solution(mesh):
    in_specs = (P("dp", None, "mp", None), P("dp", "mp", None, None, None), P("dp", None, None))
    out_specs = (P("dp", "mp", None), P("dp", "mp", None, None, None))
    return jax.shard_map(
        on_device, mesh=mesh, in_specs=in_specs, out_specs=out_specs, check_vma=False
    )
```
